1024 devices in a mesh: dp: 4 (over y_lo), expert: 32 (over z, core), shard: 8 (over x, y_hi).
Axes of the slice: x: 4, y: 8 (y_hi: 2, y_lo: 4; y = y_hi * 4 + y_lo), z: 16, core: 2. Of those that a mesh axis runs over, the one named last changes fastest.
Arguments:
- tokens: bfloat16 [32768, 2048], P(('dp', 'expert'), 'shard'), may hold values from -6 to 6
- out_grad: bfloat16 [32768, 2048], P(('dp', 'expert'), 'shard'), may hold values from -6 to 6
- expert_ids: int32 [32768, 1], P(('dp', 'expert')), may hold values from 0 to 31; in each aligned block of 256 rows (0 to 255, 256 to 511, ...) at most 16 rows name the same one
- combine: float32 [32768, 1], P(('dp', 'expert')), may hold values from 0.05 to 0.45
- old_place: int32 [32], replicated, may hold values from 0 to 31, as said below
- new_place: int32 [32], replicated, may hold values from 0 to 31
- master: float32 [32, 3, 384, 2048], P('expert', None, 'shard', 'dp'), may hold values from -0.125 to 0.125
- moment_one: float32 [32, 3, 384, 2048], P('expert', None, 'shard', 'dp'), may hold values from -4 to 4
- moment_two: float32 [32, 3, 384, 2048], P('expert', None, 'shard', 'dp'), may hold values from 0.5 to 8
Outputs:
- token_grad: bfloat16 [32768, 2048], P(('dp', 'expert'), 'shard')
- master_out: float32 [32, 3, 384, 2048], P('expert', None, 'shard', 'dp')
- first_out: float32 [32, 3, 384, 2048], P('expert', None, 'shard', 'dp')
- second_out: float32 [32, 3, 384, 2048], P('expert', None, 'shard', 'dp')
The draws below stay inside these ranges and needn't reach their ends.
Inputs may be any that keep to these rules, and one draw needn't show every extreme that they name: old_place is a permutation of the owners; new_place equals old_place except in exactly 8 entries, which hold a cyclic rotation of those entries' owners. `expert_ids`: each token names exactly one expert of the window; among the 256 rows of one block no expert is named more than 16 times, a bound that some block reaches.
All inputs are finite; a program needn't handle non-finite values.
Results may differ from the reference program's by a relative error of at most 0.012.
Values may be sent and summed in bfloat16 or wider, within the bound.
A program may use at most 32 MiB of HBM per device.

```python
import math
import jax
import jax.numpy as jnp
import numpy as np
from jax import lax

D = 2048
FF = 384
TOPW = 1
TOK_DEV = 256
EXPERTS = 32
HOT = 8
CAP = 16
TOKENS = 32768
N_DP = 4
N_EXPERT = 32
N_SHARD = 8


def placement_pair(key):
    mixed = jax.random.fold_in(key, 4242)
    key_one, key_two = jax.random.split(mixed)
    before = jax.random.permutation(key_one, EXPERTS).astype(jnp.int32)
    shuffled = jax.random.permutation(key_two, EXPERTS).astype(jnp.int32)
    moving = shuffled[:HOT]
    rotated = jnp.roll(moving, -1)
    after = before.at[moving].set(before[rotated])
    return (before, after)


def draw_old_place(key, part):
    return placement_pair(key)[0]


def draw_new_place(key, part):
    return placement_pair(key)[1]


def level_of(stream_key, shape, pieces, smallest, top_value):
    gain = 1.0
    for dim, parts in pieces:
        steps = jax.random.uniform(jax.random.fold_in(jax.random.fold_in(stream_key, 6), dim), (parts,), jnp.float32, smallest / len(pieces), top_value / len(pieces))
        gain = gain * jnp.repeat(jnp.exp(steps), shape[dim] // parts).reshape((-1,) + (1,) * (len(shape) - 1 - dim))
    return gain


def assign_block(stream_key, own, number, rows, number_of, top, most, slope):
    sequence = jax.random.permutation(stream_key, number_of)
    crowded, usual = shares(number_of, rows * top, most, slope, True), shares(number_of, rows * top, most, slope, False)
    places = jnp.arange(number_of)

    def named(lengths, offset_by):
        used = int((lengths > 0).sum())
        fixed = max(1, used // 4)
        passed = fixed + (places - fixed + offset_by * (used - fixed)) % max(1, number_of - fixed)
        return jnp.zeros((number_of,), jnp.int32).at[sequence[jnp.where(places < fixed, places, passed)]].set(jnp.asarray(lengths, jnp.int32))

    lengths = jnp.where(number % 4 == 0, named(crowded, number // 4), named(usual, number - number // 4 - 1))
    mixed = jax.random.permutation(jax.random.fold_in(own, 3), number_of)
    donor, receiver = mixed[0:number_of // 2 * 2:2], mixed[1:number_of // 2 * 2:2]
    margin = jnp.minimum(lengths[donor] - 1, most - lengths[receiver]) // 2
    margin = jnp.where((donor == sequence[0]) | (receiver == sequence[0]) | (lengths[receiver] == 0), 0, jnp.maximum(margin, 0))
    passed = jax.random.randint(jax.random.fold_in(own, 4), (number_of // 2,), 0, 1 << 20) % (margin + 1)
    lengths = lengths.at[donor].add(-passed).at[receiver].add(passed)
    items = jnp.searchsorted(jnp.cumsum(lengths), jnp.arange(rows * top), side="right").astype(jnp.int32)
    table = items.reshape(top, rows).T
    table = table[jax.random.permutation(jax.random.fold_in(own, 1), rows)]
    offset_by = jax.random.randint(jax.random.fold_in(own, 2), (rows, 1), 0, top)
    return jnp.take_along_axis(table, (jnp.arange(top)[None, :] + offset_by) % top, axis=1)


def shares(number_of, total, most, slope, full):
    loads = [(1 << 20) // math.isqrt(rank ** slope) + 1 for rank in range(1, number_of + 1)]
    largest = most if full else min(most, max(-(-total // number_of), total * loads[0] // sum(loads)))
    least = 1 if total - largest >= number_of - 1 else 0
    holding, rest = [largest] + [least] * (number_of - 1), total - largest - least * (number_of - 1)
    while rest > 0:
        free = [i for i in range(1, number_of) if holding[i] < largest] or [i for i in range(1, number_of) if holding[i] < most]
        pool, left = sum([loads[i] for i in free]), rest
        for i in free:
            extra = min(most - holding[i], max(1, left * loads[i] // pool), rest)
            holding[i] = holding[i] + extra
            rest = rest - extra
    return np.array(holding)


def noise(stream_key, dims, deviation, bound, cuts=(), kind=jnp.bfloat16):
    drawn = deviation * jax.random.normal(stream_key, dims, jnp.float32)
    if cuts:
        drawn = drawn * level_of(stream_key, dims, cuts, -0.22, 0.18)
    return jnp.clip(drawn, -bound, bound).astype(kind)


def setup_inputs(seed: int = 0) -> dict:
    streams_of = jax.random.split(jax.random.key(seed), 10)
    tokens = noise(streams_of[0], (TOKENS, D), 1.0, 6.0, ((0, 128), (1, 8)))
    out_grad = noise(streams_of[1], (TOKENS, D), 1.0, 6.0, ((0, 128), (1, 8)))
    expert_ids_keys = jax.random.split(jax.random.fold_in(streams_of[2], 1), TOKENS // TOK_DEV)
    expert_ids_turns = jax.random.permutation(jax.random.fold_in(streams_of[2], 3), TOKENS // TOK_DEV)
    expert_ids = jax.vmap(lambda own, number: assign_block(jax.random.fold_in(streams_of[2], 2), own, number, TOK_DEV, EXPERTS, TOPW, CAP, 2))(expert_ids_keys, expert_ids_turns).reshape((TOKENS, TOPW))
    combine = jnp.clip(0.05 + 0.39999999 * jax.random.uniform(streams_of[3], (TOKENS, TOPW), jnp.float32) ** level_of(streams_of[3], (TOKENS, TOPW), ((0, 128),), -0.2, 0.2), 0.05, 0.45)
    old_place = draw_old_place(jax.random.fold_in(streams_of[9], 71), 0)
    new_place = draw_new_place(jax.random.fold_in(streams_of[9], 71), 0)
    master = noise(streams_of[6], (EXPERTS, 3, FF, D), D ** -0.5, 0.125, ((0, 32), (2, 8), (3, 4)), jnp.float32)
    moment_one = noise(streams_of[7], (EXPERTS, 3, FF, D), 0.5, 4.0, ((0, 32), (2, 8), (3, 4)), jnp.float32)
    moment_two = jnp.clip(jnp.exp(math.log(8.0) - 2.7725887 * jax.random.uniform(streams_of[8], (EXPERTS, 3, FF, D), jnp.float32) ** level_of(streams_of[8], (EXPERTS, 3, FF, D), ((0, 32), (2, 8), (3, 4)), -0.2, 0.2)), 0.5, 8.0)
    return dict(tokens=tokens, out_grad=out_grad, expert_ids=expert_ids, combine=combine, old_place=old_place, new_place=new_place, master=master, moment_one=moment_one, moment_two=moment_two)


beta_first = 0.9
beta_second = 0.95
adam_epsilon = 1e-08
learn_rate = 0.001
weight_decay = 0.1
bias_first = 1.0 - beta_first ** 10
bias_second = 1.0 - beta_second ** 10

def adamw_step(master, moment_one, moment_two, gradient):
    first_out = beta_first * moment_one + (1.0 - beta_first) * gradient
    second_out = beta_second * moment_two + (1.0 - beta_second) * gradient * gradient
    update = first_out / bias_first / (jnp.sqrt(second_out / bias_second) + adam_epsilon)
    master_out = master - learn_rate * (update + weight_decay * master)
    return (master_out, first_out, second_out)

def reference(tokens, out_grad, expert_ids, combine, old_place, new_place, master, moment_one, moment_two):
    owners = jnp.arange(EXPERTS, dtype=jnp.int32)
    holds = (new_place[:, None] == owners[None, :]).astype(jnp.int32)
    source_owner = lax.optimization_barrier(jnp.sum(old_place[:, None] * holds, axis=0)).astype(jnp.int32)
    moved_master = master[source_owner]
    moved_one = moment_one[source_owner]
    moved_two = moment_two[source_owner]
    weights = moved_master.astype(jnp.bfloat16)
    blocks = N_DP * N_EXPERT
    assign = TOK_DEV * TOPW
    flat_ids = expert_ids.reshape(blocks, assign)
    onehot = (flat_ids[:, :, None] == owners[None, None, :]).astype(jnp.int32)
    earlier = jnp.cumsum(onehot, axis=1) - onehot
    slot = lax.optimization_barrier(jnp.sum(earlier * onehot, axis=2)).astype(jnp.int32)
    target = lax.optimization_barrier(jnp.sum(onehot * new_place[None, None, :], axis=2)).astype(jnp.int32)
    block_index = jnp.arange(blocks, dtype=jnp.int32)[:, None]
    replica = block_index // N_EXPERT
    sender = block_index % N_EXPERT
    position = ((target * N_DP + replica) * N_EXPERT + sender) * CAP + slot
    token_index = block_index * TOK_DEV + jnp.arange(assign, dtype=jnp.int32)[None, :] // TOPW
    row_count = N_DP * N_EXPERT * CAP
    table = jnp.zeros((EXPERTS * row_count,), jnp.int32).at[position.reshape(-1)].set(token_index.reshape(-1) + 1)
    scales = jnp.zeros((EXPERTS * row_count,), jnp.float32).at[position.reshape(-1)].set(combine.reshape(-1))
    table = table.reshape(EXPERTS, row_count)
    scales = scales.reshape(EXPERTS, row_count)
    width_f = FF // N_SHARD

    def per_owner(inputs):
        row_table, row_scale, weight, master_own, first_own, second_own = inputs
        valid = row_table > 0
        picked = jnp.maximum(row_table - 1, 0)
        rows_x = jnp.where(valid[:, None], tokens[picked], jnp.zeros((), jnp.bfloat16)).astype(jnp.bfloat16)
        rows_dy = jnp.where(valid[:, None], row_scale[:, None] * out_grad[picked].astype(jnp.float32), jnp.zeros((), jnp.float32)).astype(jnp.bfloat16)
        gate_pre = jnp.dot(rows_x, weight[0].T, preferred_element_type=jnp.float32)
        up_pre = jnp.dot(rows_x, weight[1].T, preferred_element_type=jnp.float32)
        sigma = jax.nn.sigmoid(gate_pre)
        active = gate_pre * sigma
        hidden = (active * up_pre).astype(jnp.bfloat16)
        grad_hidden = jnp.dot(rows_dy, weight[2].T, preferred_element_type=jnp.float32)
        grad_up = (grad_hidden * active).astype(jnp.bfloat16)
        grad_gate = (grad_hidden * up_pre * sigma * (1.0 + gate_pre * (1.0 - sigma))).astype(jnp.bfloat16)
        gate_groups = grad_gate.reshape(row_count, N_SHARD, width_f).astype(jnp.float32)
        up_groups = grad_up.reshape(row_count, N_SHARD, width_f).astype(jnp.float32)
        gate_table = weight[0].reshape(N_SHARD, width_f, D).astype(jnp.float32)
        up_table = weight[1].reshape(N_SHARD, width_f, D).astype(jnp.float32)
        group_terms = jnp.einsum('rsf,sfd->srd', gate_groups, gate_table) + jnp.einsum('rsf,sfd->srd', up_groups, up_table)
        group_terms = lax.optimization_barrier(group_terms.astype(jnp.bfloat16))
        row_grad = lax.optimization_barrier(jnp.sum(group_terms.astype(jnp.float32), axis=0))
        x_rep = rows_x.reshape(N_DP, -1, D).astype(jnp.float32)
        dy_rep = rows_dy.reshape(N_DP, -1, D).astype(jnp.float32)
        gate_rep = grad_gate.reshape(N_DP, -1, FF).astype(jnp.float32)
        up_rep = grad_up.reshape(N_DP, -1, FF).astype(jnp.float32)
        hidden_rep = hidden.reshape(N_DP, -1, FF).astype(jnp.float32)
        replica_grad = jnp.stack([jnp.einsum('prf,prd->pfd', gate_rep, x_rep), jnp.einsum('prf,prd->pfd', up_rep, x_rep), jnp.einsum('prf,prd->pfd', hidden_rep, dy_rep)], axis=1)
        replica_grad = lax.optimization_barrier(replica_grad.astype(jnp.bfloat16))
        gradient = lax.optimization_barrier(jnp.sum(replica_grad.astype(jnp.float32), axis=0))
        master_new, first_new, second_new = adamw_step(master_own, first_own, second_own, gradient)
        return (row_grad, master_new, first_new, second_new)
    row_grads, master_out, first_out, second_out = lax.map(per_owner, (table, scales, weights, moved_master, moved_one, moved_two))
    where_to = jnp.where(table > 0, table - 1, TOKENS).astype(jnp.int32).reshape(-1)
    token_grad = jnp.zeros((TOKENS, D), jnp.float32).at[where_to].add(row_grads.reshape(-1, D), mode='drop')
    return (token_grad.astype(jnp.bfloat16), master_out, first_out, second_out)
```

```python
import functools

import jax
import jax.numpy as jnp
from jax import lax
from jax.experimental import pallas as pl
from jax.experimental.pallas import tpu as pltpu
from jax.sharding import PartitionSpec as P

MESH = pl.DeviceIdType.MESH
bf16 = jnp.bfloat16
f32 = jnp.float32

beta_first = 0.9
beta_second = 0.95
adam_epsilon = 1e-08
learn_rate = 0.001
weight_decay = 0.1
bias_first = 1.0 - beta_first**10
bias_second = 1.0 - beta_second**10

CHUNKS = 4
CAP = 16
PARKS = ((0, 0), (0, 1), (2, 0))


def same_bytes(ref, sem):
    return pltpu.make_async_copy(ref, ref, sem)


def adamw_step(master, moment_one, moment_two, gradient):
    first_out = beta_first * moment_one + (1.0 - beta_first) * gradient
    second_out = beta_second * moment_two + (1.0 - beta_second) * gradient * gradient
    update = first_out / bias_first / (jnp.sqrt(second_out / bias_second) + adam_epsilon)
    master_out = master - learn_rate * (update + weight_decay * master)
    return master_out, first_out, second_out


def kernel(
    source_ref, place_ref, ids_ref, combine_ref, tokens_ref, out_grad_ref,
    master_ref, one_ref, two_ref,
    token_grad_ref, master_out_ref, first_out_ref, second_out_ref,
    match, rows_out, rows_in, states, parked, onward, moved,
    weight, partial, rs, yb, yr, act, row_grad, returned, wgrad, grads,
    send_sem, rows_sem, park_sem, moved_sem, weight_sem, rs_sem, y_sem, ag_sem, ret_sem, grad_sem,
):
    p = lax.axis_index("dp")
    me = lax.axis_index("expert")
    s = lax.axis_index("shard")
    z, core = me // 2, me % 2
    x, yh = s // 2, s % 2
    n_owner = 32
    n_rows = n_owner * CAP
    chunk_rows = n_rows // CHUNKS
    block_rows = chunk_rows // 4
    width = tokens_ref.shape[1]
    ff = weight.shape[1]
    part_ff = ff // 8

    barrier = pltpu.get_barrier_semaphore()

    def greet(device):
        pl.semaphore_signal(barrier, inc=1, device_id=device, device_id_type=MESH)

    def greet_owner(i, c):
        greet({"expert": (me + i) % n_owner})
        return c

    lax.fori_loop(1, n_owner, greet_owner, 0)
    for j in (1, 2, 3):
        greet({"shard": ((x + j) % 4) * 2 + yh})
    greet({"shard": x * 2 + 1 - yh})
    diagonal = x == p

    def greet_spread(i, c):
        h, q = i // 4, i % 4

        @pl.when(jnp.logical_or(q != p, p * 2 + h != s))
        def _():
            greet({"dp": q, "shard": p * 2 + h})

        @pl.when(jnp.logical_or(x != p, i != s))
        def _():
            greet({"dp": x, "shard": i})

        return c

    lax.fori_loop(0, 8, greet_spread, 0)
    states[0] = master_ref[0].astype(bf16)
    pl.semaphore_wait(barrier, jnp.where(diagonal, 49, 51))

    def park_device(a, k):
        shift, c = PARKS[a]
        return 2 * ((k + k // 3 + shift) % 16) + c

    def is_park(a):
        shift, c = PARKS[a]
        zz = (z + 16 - shift) % 16
        return jnp.logical_and(core == c, zz % 4 != 3), zz - zz // 4

    def park(a):
        def step(k, c):
            g, lane = k // 4, pl.multiple_of((k % 4) * 128, 128)
            dest = park_device(a, k)
            src = states.at[a, g, :, pl.ds(lane, 128)]

            @pl.when(dest != me)
            def _():
                pltpu.make_async_remote_copy(
                    src_ref=src, dst_ref=parked.at[a, me], send_sem=send_sem.at[a],
                    recv_sem=park_sem.at[a], device_id={"expert": dest}, device_id_type=MESH,
                ).start()

            @pl.when(dest == me)
            def _():
                pltpu.make_async_copy(src, parked.at[a, me], park_sem.at[a]).start()

            return c

        lax.fori_loop(0, 12, step, 0)

    def send_on(a):
        mine, k = is_park(a)
        g, lane = k // 4, pl.multiple_of((k % 4) * 128, 128)

        @pl.when(mine)
        def _():
            same_bytes(parked.at[a], park_sem.at[a]).wait()

            def step(i, c):
                o = (me + i) % n_owner
                onward[a, o] = parked[a, source_ref[o]]
                dst = moved.at[a, g, :, pl.ds(lane, 128)]

                @pl.when(i != 0)
                def _():
                    pltpu.make_async_remote_copy(
                        src_ref=onward.at[a, o], dst_ref=dst, send_sem=send_sem.at[3 + a],
                        recv_sem=moved_sem.at[a], device_id={"expert": o}, device_id_type=MESH,
                    ).start()

                @pl.when(i == 0)
                def _():
                    pltpu.make_async_copy(onward.at[a, o], dst, moved_sem.at[a]).start()

                return c

            lax.fori_loop(0, n_owner, step, 0)

    def states_sent(a):
        mine, _ = is_park(a)

        @pl.when(mine)
        def _():
            same_bytes(onward.at[a, pl.ds(0, 11)], send_sem.at[a]).wait()
            same_bytes(onward.at[a, pl.ds(0, 31)], send_sem.at[3 + a]).wait()

        @pl.when(jnp.logical_not(mine))
        def _():
            same_bytes(onward.at[a, pl.ds(0, 12)], send_sem.at[a]).wait()

    park(0)

    tok = tokens_ref.shape[0]
    eye = lax.broadcasted_iota(jnp.int32, (n_owner, n_owner), 0) == lax.broadcasted_iota(
        jnp.int32, (n_owner, n_owner), 1
    )
    place = jnp.sum(jnp.where(eye, place_ref[...].astype(f32), 0.0), axis=1, keepdims=True)
    onehot = jnp.where(
        lax.broadcasted_iota(jnp.int32, (n_owner, tok), 0) == ids_ref[...], 1.0, 0.0
    )
    before = jnp.where(
        lax.broadcasted_iota(jnp.int32, (tok, tok), 0) < lax.broadcasted_iota(jnp.int32, (tok, tok), 1),
        1.0, 0.0,
    ).astype(bf16)
    earlier = jnp.dot(onehot.astype(bf16), before, preferred_element_type=f32)
    position = jnp.sum(onehot * (earlier + place * float(CAP)), axis=0, keepdims=True)
    chosen = lax.broadcasted_iota(jnp.int32, (n_rows, tok), 0).astype(f32) == position
    match[...] = jnp.where(chosen, 1.0, 0.0).astype(bf16)
    scale = jnp.sum(jnp.where(chosen, combine_ref[...], 0.0), axis=1, keepdims=True)
    rows_out[:, :width] = jnp.dot(match[...], tokens_ref[...], preferred_element_type=f32).astype(bf16)
    rows_out[:, width:] = (
        scale * jnp.dot(match[...], out_grad_ref[...], preferred_element_type=f32)
    ).astype(bf16)

    send_on(0)

    def dz_of(rank):
        return jnp.where(rank % 2 == 1, (rank + 1) // 2, (16 - rank // 2) % 16)

    def dispatch(i, c):
        rank, to_core = i // 2, i % 2
        dest = ((z + 16 - dz_of(rank)) % 16) * 2 + to_core
        src = rows_out.at[pl.ds(pl.multiple_of(dest * CAP, CAP), CAP), :]
        dst = rows_in.at[pl.ds(pl.multiple_of((rank * 2 + core) * CAP, CAP), CAP), :]
        sem = rows_sem.at[rank // (16 // CHUNKS)]

        @pl.when(dest != me)
        def _():
            pltpu.make_async_remote_copy(
                src_ref=src, dst_ref=dst, send_sem=send_sem.at[6], recv_sem=sem,
                device_id={"expert": dest}, device_id_type=MESH,
            ).start()

        @pl.when(dest == me)
        def _():
            pltpu.make_async_copy(src, dst, sem).start()

        return c

    lax.fori_loop(0, n_owner, dispatch, 0)

    same_bytes(moved.at[0], moved_sem.at[0]).wait()

    def spread(i, c):
        h, q = i // 4, i % 4
        src = moved.at[0, :, :, pl.ds(pl.multiple_of(h * width, width), width)]
        dst = weight.at[:, pl.ds(pl.multiple_of(s * part_ff, 16), part_ff), :]
        away = jnp.logical_or(q != p, p * 2 + h != s)

        @pl.when(away)
        def _():
            pltpu.make_async_remote_copy(
                src_ref=src, dst_ref=dst, send_sem=send_sem.at[7], recv_sem=weight_sem,
                device_id={"dp": q, "shard": p * 2 + h}, device_id_type=MESH,
            ).start()

        @pl.when(jnp.logical_not(away))
        def _():
            pltpu.make_async_copy(src, dst, weight_sem).start()

        return c

    lax.fori_loop(0, 8, spread, 0)
    states[1] = one_ref[0].astype(bf16)
    states[2] = two_ref[0].astype(bf16)
    same_bytes(weight, weight_sem).wait()

    def products(c):
        same_bytes(rows_in.at[pl.ds(c * chunk_rows, chunk_rows)], rows_sem.at[c]).wait()
        rows = rows_in[pl.ds(c * chunk_rows, chunk_rows), :]
        nt = (((1,), (1,)), ((), ()))
        here = pl.ds(c * chunk_rows, chunk_rows)
        for g in range(3):
            lhs = rows[:, :width] if g < 2 else rows[:, width:]
            partial[here, g * ff : (g + 1) * ff] = lax.dot_general(
                lhs, weight[g], nt, preferred_element_type=f32
            ).astype(bf16)
        for j in (1, 2, 3):
            xx = (x + j) % 4
            pltpu.make_async_remote_copy(
                src_ref=partial.at[pl.ds(pl.multiple_of(c * chunk_rows + xx * block_rows, 16), block_rows), :],
                dst_ref=rs.at[c, j - 1], send_sem=send_sem.at[8], recv_sem=rs_sem.at[c],
                device_id={"shard": xx * 2 + yh}, device_id_type=MESH,
            ).start()

    def own_rows(c):
        return pl.ds(pl.multiple_of(c * chunk_rows + x * block_rows, 16), block_rows)

    def half_sums(c):
        same_bytes(rs.at[c], rs_sem.at[c]).wait()
        total = partial[own_rows(c), :].astype(f32)
        for j in range(3):
            total += rs[c, j].astype(f32)
        yb[c] = total.astype(bf16)
        pltpu.make_async_remote_copy(
            src_ref=yb.at[c], dst_ref=yr.at[c], send_sem=send_sem.at[9], recv_sem=y_sem.at[c],
            device_id={"shard": x * 2 + 1 - yh}, device_id_type=MESH,
        ).start()

    def activations(c):
        same_bytes(yr.at[c], y_sem.at[c]).wait()
        total = yb[c].astype(f32) + yr[c].astype(f32)
        gate, up, grad_hidden = total[:, :ff], total[:, ff : 2 * ff], total[:, 2 * ff :]
        sigma = jax.nn.sigmoid(gate)
        active = gate * sigma
        here = own_rows(c)
        act[here, :ff] = (grad_hidden * up * sigma * (1.0 + gate * (1.0 - sigma))).astype(bf16)
        act[here, ff : 2 * ff] = (grad_hidden * active).astype(bf16)
        act[here, 2 * ff :] = (active * up).astype(bf16)
        for j in (1, 2, 3):
            xx = (x + j) % 4
            pltpu.make_async_remote_copy(
                src_ref=act.at[here, :], dst_ref=act.at[here, :], send_sem=send_sem.at[10],
                recv_sem=ag_sem.at[c], device_id={"shard": xx * 2 + yh}, device_id_type=MESH,
            ).start()

    def gathered(c):
        same_bytes(rs.at[c], ag_sem.at[c]).wait()

    def row_grads(c):
        here = pl.ds(c * chunk_rows, chunk_rows)
        row_grad[here, :] = (
            jnp.dot(act[here, :ff], weight[0], preferred_element_type=f32)
            + jnp.dot(act[here, ff : 2 * ff], weight[1], preferred_element_type=f32)
        ).astype(bf16)

        def give_back(i, carry):
            rank, to_core = i // 2, i % 2
            dest = ((z + dz_of(rank)) % 16) * 2 + to_core
            src = row_grad.at[pl.ds(pl.multiple_of(i * CAP, CAP), CAP), :]
            dst = returned.at[pl.ds(pl.multiple_of(me * CAP, CAP), CAP), :]

            @pl.when(dest != me)
            def _():
                pltpu.make_async_remote_copy(
                    src_ref=src, dst_ref=dst, send_sem=send_sem.at[11], recv_sem=ret_sem,
                    device_id={"expert": dest}, device_id_type=MESH,
                ).start()

            @pl.when(dest == me)
            def _():
                pltpu.make_async_copy(src, dst, ret_sem).start()

            return carry

        lax.fori_loop(c * (n_owner // CHUNKS), (c + 1) * (n_owner // CHUNKS), give_back, 0)

    for step in range(CHUNKS + 2):
        if step < CHUNKS:
            products(step)
        if step == CHUNKS - 1:
            park(1)
            park(2)
        if 0 <= step - 1 < CHUNKS:
            half_sums(step - 1)
        if 0 <= step - 2 < CHUNKS:
            activations(step - 2)
    send_on(1)
    send_on(2)
    for c in range(CHUNKS - 1):
        gathered(c)
        row_grads(c)
    gathered(CHUNKS - 1)

    tn = (((0,), (0,)), ((), ()))
    for g in range(3):
        right = rows_in[:, :width] if g < 2 else rows_in[:, width:]
        wgrad[g] = lax.dot_general(
            act[:, g * ff : (g + 1) * ff], right, tn, preferred_element_type=f32
        ).astype(bf16)

    def to_holder(i, c):
        src = wgrad.at[:, pl.ds(pl.multiple_of(i * part_ff, 16), part_ff), :]
        dst = grads.at[yh * 4 + p]
        away = jnp.logical_or(x != p, i != s)

        @pl.when(away)
        def _():
            pltpu.make_async_remote_copy(
                src_ref=src, dst_ref=dst, send_sem=send_sem.at[12], recv_sem=grad_sem,
                device_id={"dp": x, "shard": i}, device_id_type=MESH,
            ).start()

        @pl.when(jnp.logical_not(away))
        def _():
            pltpu.make_async_copy(src, dst, grad_sem).start()

        return c

    lax.fori_loop(0, 8, to_holder, 0)
    row_grads(CHUNKS - 1)

    same_bytes(returned, ret_sem).wait()
    token_grad_ref[...] = lax.dot_general(
        match[...], returned[...], tn, preferred_element_type=f32
    ).astype(bf16)

    same_bytes(moved.at[1], moved_sem.at[1]).wait()
    same_bytes(moved.at[2], moved_sem.at[2]).wait()
    same_bytes(grads, grad_sem).wait()
    for h in range(2):
        half = slice(h * width, (h + 1) * width)
        for g in range(3):
            gradient = grads[h * 4, g].astype(f32)
            for q in range(1, 4):
                gradient += grads[h * 4 + q, g].astype(f32)
            a, b, d = adamw_step(
                moved[0, g, :, half].astype(f32), moved[1, g, :, half].astype(f32),
                moved[2, g, :, half].astype(f32), gradient,
            )
            master_out_ref[0, g, :, half] = a
            first_out_ref[0, g, :, half] = b
            second_out_ref[0, g, :, half] = d

    for a in range(3):
        states_sent(a)
    same_bytes(rows_out.at[pl.ds(0, 31 * CAP)], send_sem.at[6]).wait()
    for index, buffer in ((7, moved.at[0]), (12, wgrad)):
        @pl.when(diagonal)
        def _(index=index):
            same_bytes(grads.at[pl.ds(0, 7)], send_sem.at[index]).wait()

        @pl.when(jnp.logical_not(diagonal))
        def _(index=index):
            same_bytes(grads, send_sem.at[index]).wait()
    same_bytes(rs, send_sem.at[8]).wait()
    same_bytes(yb, send_sem.at[9]).wait()
    same_bytes(rs, send_sem.at[10]).wait()
    same_bytes(row_grad.at[pl.ds(0, 31 * CAP)], send_sem.at[11]).wait()


def on_device(
    tokens, out_grad, expert_ids, combine, old_place, new_place, master, moment_one, moment_two
):
    n_owner = 32
    owners = jnp.arange(n_owner, dtype=jnp.int32)
    holds = (new_place[:, None] == owners[None, :]).astype(jnp.int32)
    source_owner = jnp.sum(old_place[:, None] * holds, axis=0)
    tok, width = tokens.shape
    _, mats, part_ff, held_width = master.shape
    ff = part_ff * 8
    rows = n_owner * CAP
    block = rows // CHUNKS // 4
    vmem = pl.BlockSpec(memory_space=pltpu.VMEM)
    dma = pltpu.SemaphoreType.DMA
    return pl.pallas_call(
        kernel,
        out_shape=(
            jax.ShapeDtypeStruct(tokens.shape, bf16),
            jax.ShapeDtypeStruct(master.shape, f32),
            jax.ShapeDtypeStruct(master.shape, f32),
            jax.ShapeDtypeStruct(master.shape, f32),
        ),
        in_specs=[pl.BlockSpec(memory_space=pltpu.SMEM)] + [vmem] * 8,
        out_specs=(vmem,) * 4,
        scratch_shapes=[
            pltpu.VMEM((rows, tok), bf16),
            pltpu.VMEM((rows, 2 * width), bf16),
            pltpu.VMEM((rows, 2 * width), bf16),
            pltpu.VMEM((3, mats, part_ff, held_width), bf16),
            pltpu.VMEM((3, n_owner, part_ff, 128), bf16),
            pltpu.VMEM((3, n_owner, part_ff, 128), bf16),
            pltpu.VMEM((3, mats, part_ff, held_width), bf16),
            pltpu.VMEM((mats, ff, width), bf16),
            pltpu.VMEM((rows, 3 * ff), bf16),
            pltpu.VMEM((CHUNKS, 3, block, 3 * ff), bf16),
            pltpu.VMEM((CHUNKS, block, 3 * ff), bf16),
            pltpu.VMEM((CHUNKS, block, 3 * ff), bf16),
            pltpu.VMEM((rows, 3 * ff), bf16),
            pltpu.VMEM((rows, width), bf16),
            pltpu.VMEM((rows, width), bf16),
            pltpu.VMEM((mats, ff, width), bf16),
            pltpu.VMEM((8, mats, part_ff, width), bf16),
            dma((13,)),
            dma((CHUNKS,)),
            dma((3,)),
            dma((3,)),
            dma,
            dma((CHUNKS,)),
            dma((CHUNKS,)),
            dma((CHUNKS,)),
            dma,
            dma,
        ],
        compiler_params=pltpu.CompilerParams(
            collective_id=0, has_side_effects=True, vmem_limit_bytes=40 * 1024 * 1024
        ),
    )(
        source_owner, new_place.reshape(1, n_owner), expert_ids.reshape(1, tok),
        combine.reshape(1, tok), tokens, out_grad, master, moment_one, moment_two,
    )


def solution(mesh):
    in_specs = (
        P(("dp", "expert"), "shard"),
        P(("dp", "expert"), "shard"),
        P(("dp", "expert"), None),
        P(("dp", "expert"), None),
        P(),
        P(),
        P("expert", None, "shard", "dp"),
        P("expert", None, "shard", "dp"),
        P("expert", None, "shard", "dp"),
    )
    out_specs = (
        P(("dp", "expert"), "shard"),
        P("expert", None, "shard", "dp"),
        P("expert", None, "shard", "dp"),
        P("expert", None, "shard", "dp"),
    )
    return jax.shard_map(
        on_device, mesh=mesh, in_specs=in_specs, out_specs=out_specs, check_vma=False
    )
```

```python
import functools

import jax
import jax.numpy as jnp
from jax import lax
from jax.experimental import pallas as pl
from jax.experimental.pallas import tpu as pltpu
from jax.sharding import PartitionSpec as P

MESH = pl.DeviceIdType.MESH
bf16 = jnp.bfloat16
f32 = jnp.float32

beta_first = 0.9
beta_second = 0.95
adam_epsilon = 1e-08
learn_rate = 0.001
weight_decay = 0.1
bias_first = 1.0 - beta_first**10
bias_second = 1.0 - beta_second**10

LAG_SUM, LAG_ACT = 4, 8
AT_ONE, AT_TWO, AT_TURN = 8, 10, 13
CHUNKS = 4
CAP = 16
PARKS = ((0, 0), (0, 1), (2, 0))


def same_bytes(ref, sem):
    return pltpu.make_async_copy(ref, ref, sem)


def adamw_step(master, moment_one, moment_two, gradient):
    first_out = beta_first * moment_one + (1.0 - beta_first) * gradient
    second_out = beta_second * moment_two + (1.0 - beta_second) * gradient * gradient
    update = first_out / bias_first / (jnp.sqrt(second_out / bias_second) + adam_epsilon)
    master_out = master - learn_rate * (update + weight_decay * master)
    return master_out, first_out, second_out


def kernel(
    source_ref, *refs,
):
    inputs, outputs, scratch = refs[:8], refs[8:12], refs[12:]
    body(source_ref, inputs, *outputs, *scratch)


def body(
    source_ref, inputs,
    token_grad_ref, master_out_ref, first_out_ref, second_out_ref,
    place_ref, ids_ref, combine_ref, tokens_ref, out_grad_ref, master_ref, one_ref, two_ref,
    match, rows_out, rows_in, states, parked_0, parked_1, parked_2, onward, moved,
    weight, partial_gu, partial_dn, rs_gu, rs_dn, yb_gu, yb_dn, yr_gu, yr_dn, act_hid, act_gu, row_grad, returned, wgrad, turned, grads,
    in_sem, send_sem, rows_sem, park_sem, moved_sem, weight_sem, rs_sem, y_sem, ag_sem, ret_sem, turn_sem, grad_sem,
):
    p = lax.axis_index("dp")
    me = lax.axis_index("expert")
    s = lax.axis_index("shard")
    z, core = me // 2, me % 2
    x, yh = s // 2, s % 2
    n_owner = 32
    n_rows = n_owner * CAP
    chunk_rows = n_rows // CHUNKS
    block_rows = chunk_rows // 4
    width = tokens_ref.shape[1]
    ff = weight.shape[1]
    part_ff = ff // 8

    y = yh * 4 + p
    parked = (parked_0, parked_1, parked_2)
    staged = (place_ref, ids_ref, combine_ref, tokens_ref, out_grad_ref, master_ref, one_ref, two_ref)

    def load(i):
        return pltpu.make_async_copy(inputs[i], staged[i], in_sem.at[i])

    for i in (5, 0, 1, 2, 3, 4, 6, 7):
        load(i).start()

    def offset(n, i):
        rank = n - 1 - i
        return jnp.where(rank % 2 == 1, (rank + 1) // 2, (n - rank // 2) % n)

    barrier = pltpu.get_barrier_semaphore()

    def greet(device):
        pl.semaphore_signal(barrier, inc=1, device_id=device, device_id_type=MESH)

    def greet_owner(i, c):
        greet({"expert": (me + i) % n_owner})
        return c

    lax.fori_loop(1, n_owner, greet_owner, 0)
    for j in (1, 2, 3):
        greet({"shard": ((x + j) % 4) * 2 + yh})

    def greet_y(i, c):
        to = (y + i) % 8
        greet({"dp": to % 4, "shard": x * 2 + to // 4})
        return c

    lax.fori_loop(1, 8, greet_y, 0)
    diagonal = x == p

    def greet_spread(i, c):
        h, q = i // 4, i % 4

        @pl.when(jnp.logical_or(q != p, p * 2 + h != s))
        def _():
            greet({"dp": q, "shard": p * 2 + h})

        @pl.when(jnp.logical_or(x != p, i != s))
        def _():
            greet({"dp": x, "shard": i})

        return c

    lax.fori_loop(0, 8, greet_spread, 0)
    load(5).wait()
    states[0] = master_ref[0].astype(bf16)
    pl.semaphore_wait(barrier, jnp.where(diagonal, 55, 57))

    def is_park(a):
        shift, c = PARKS[a]
        zz = (z + 16 - shift) % 16
        return jnp.logical_and(core == c, zz % 4 != 3), jnp.minimum(zz - zz // 4, 11)

    def park(a):
        shift, to_core = PARKS[a]

        def step(i, c):
            to = (z + offset(16, i)) % 16
            place_in = (to + 16 - shift) % 16
            k = jnp.minimum(place_in - place_in // 4, 11)
            g, lane = k // 4, pl.multiple_of((k % 4) * 128, 128)
            dest = 2 * to + to_core
            holds_one = place_in % 4 != 3
            src = states.at[a, g, :, pl.ds(lane, 128)]

            @pl.when(jnp.logical_and(holds_one, dest != me))
            def _():
                pltpu.make_async_remote_copy(
                    src_ref=src, dst_ref=parked[a].at[me], send_sem=send_sem.at[a],
                    recv_sem=park_sem.at[a], device_id={"expert": dest}, device_id_type=MESH,
                ).start()

            @pl.when(jnp.logical_and(holds_one, dest == me))
            def _():
                pltpu.make_async_copy(src, parked[a].at[me], park_sem.at[a]).start()

            return c

        lax.fori_loop(0, 16, step, 0)

    def send_on(a):
        mine, k = is_park(a)
        g, lane = k // 4, pl.multiple_of((k % 4) * 128, 128)

        @pl.when(mine)
        def _():
            same_bytes(parked[a], park_sem.at[a]).wait()

            def step(i, c):
                o = ((z + offset(16, i // 2)) % 16) * 2 + i % 2
                onward[a, o] = parked[a][source_ref[o]]
                dst = moved.at[a, g, :, pl.ds(lane, 128)]

                @pl.when(o != me)
                def _():
                    pltpu.make_async_remote_copy(
                        src_ref=onward.at[a, o], dst_ref=dst, send_sem=send_sem.at[3 + a],
                        recv_sem=moved_sem.at[a], device_id={"expert": o}, device_id_type=MESH,
                    ).start()

                @pl.when(o == me)
                def _():
                    pltpu.make_async_copy(onward.at[a, o], dst, moved_sem.at[a]).start()

                return c

            lax.fori_loop(0, n_owner, step, 0)

    def states_sent(a):
        mine, _ = is_park(a)

        @pl.when(mine)
        def _():
            same_bytes(onward.at[a, pl.ds(0, 11)], send_sem.at[a]).wait()
            same_bytes(onward.at[a, pl.ds(0, 31)], send_sem.at[3 + a]).wait()

        @pl.when(jnp.logical_not(mine))
        def _():
            same_bytes(onward.at[a, pl.ds(0, 12)], send_sem.at[a]).wait()

    park(0)

    for i in range(5):
        load(i).wait()
    tok = tokens_ref.shape[0]
    eye = lax.broadcasted_iota(jnp.int32, (n_owner, n_owner), 0) == lax.broadcasted_iota(
        jnp.int32, (n_owner, n_owner), 1
    )
    place = jnp.sum(jnp.where(eye, place_ref[...].astype(f32), 0.0), axis=1, keepdims=True)
    onehot = jnp.where(
        lax.broadcasted_iota(jnp.int32, (n_owner, tok), 0) == ids_ref[...], 1.0, 0.0
    )
    before = jnp.where(
        lax.broadcasted_iota(jnp.int32, (tok, tok), 0) < lax.broadcasted_iota(jnp.int32, (tok, tok), 1),
        1.0, 0.0,
    ).astype(bf16)
    earlier = jnp.dot(onehot.astype(bf16), before, preferred_element_type=f32)
    position = jnp.sum(onehot * (earlier + place * float(CAP)), axis=0, keepdims=True)
    chosen = lax.broadcasted_iota(jnp.int32, (n_rows, tok), 0).astype(f32) == position
    match[...] = jnp.where(chosen, 1.0, 0.0).astype(bf16)
    scale = jnp.sum(jnp.where(chosen, combine_ref[...], 0.0), axis=1, keepdims=True)
    rows_out[:, :width] = jnp.dot(match[...], tokens_ref[...], preferred_element_type=f32).astype(bf16)
    rows_out[:, width:] = (
        scale * jnp.dot(match[...], out_grad_ref[...], preferred_element_type=f32)
    ).astype(bf16)

    send_on(0)

    def dispatch(i, c):
        rank, to_core = i // 2, i % 2
        dest = ((z + 16 - offset(16, rank)) % 16) * 2 + to_core
        src = rows_out.at[pl.ds(pl.multiple_of(dest * CAP, CAP), CAP), :]
        dst = rows_in.at[pl.ds(pl.multiple_of((rank * 2 + core) * CAP, CAP), CAP), :]
        sem = rows_sem.at[rank // (16 // CHUNKS)]

        @pl.when(dest != me)
        def _():
            pltpu.make_async_remote_copy(
                src_ref=src, dst_ref=dst, send_sem=send_sem.at[6], recv_sem=sem,
                device_id={"expert": dest}, device_id_type=MESH,
            ).start()

        @pl.when(dest == me)
        def _():
            pltpu.make_async_copy(src, dst, sem).start()

        return c

    lax.fori_loop(0, n_owner, dispatch, 0)

    same_bytes(moved.at[0], moved_sem.at[0]).wait()

    def spread_part(part, i, c):
        to = (y + offset(8, i)) % 8
        h, q = to // 4, to % 4
        mats = pl.ds(0, 2) if part == 0 else pl.ds(2, 1)
        src = moved.at[0, mats, :, pl.ds(pl.multiple_of(h * width, width), width)]
        dst = weight.at[mats, pl.ds(pl.multiple_of(s * part_ff, 16), part_ff), :]
        away = jnp.logical_or(q != p, p * 2 + h != s)

        @pl.when(away)
        def _():
            pltpu.make_async_remote_copy(
                src_ref=src, dst_ref=dst, send_sem=send_sem.at[7], recv_sem=weight_sem.at[part],
                device_id={"dp": q, "shard": p * 2 + h}, device_id_type=MESH,
            ).start()

        @pl.when(jnp.logical_not(away))
        def _():
            pltpu.make_async_copy(src, dst, weight_sem.at[part]).start()

        return c

    lax.fori_loop(0, 8, functools.partial(spread_part, 0), 0)
    lax.fori_loop(0, 8, functools.partial(spread_part, 1), 0)
    load(6).wait()
    states[1] = one_ref[0].astype(bf16)
    park(1)
    load(7).wait()
    states[2] = two_ref[0].astype(bf16)
    park(2)
    same_bytes(weight.at[pl.ds(0, 2)], weight_sem.at[0]).wait()

    nt = (((1,), (1,)), ((), ()))

    def own_rows(c):
        return pl.ds(pl.multiple_of(c * chunk_rows + x * block_rows, 16), block_rows)

    sides = (
        (partial_gu, rs_gu, yb_gu, yr_gu, act_hid, rs_dn),
        (partial_dn, rs_dn, yb_dn, yr_dn, act_gu, rs_gu),
    )

    def products(part, c):
        partial, rs = sides[part][:2]
        unit = part * CHUNKS + c
        here = pl.ds(c * chunk_rows, chunk_rows)
        if part == 0:
            same_bytes(rows_in.at[here], rows_sem.at[c]).wait()
            for g in range(2):
                partial[here, g * ff : (g + 1) * ff] = lax.dot_general(
                    rows_in[here, :width], weight[g], nt, preferred_element_type=f32
                ).astype(bf16)
        else:
            partial[here, :] = lax.dot_general(
                rows_in[here, width:], weight[2], nt, preferred_element_type=f32
            ).astype(bf16)
        for j in (2, 1, 3):
            xx = (x + j) % 4
            pltpu.make_async_remote_copy(
                src_ref=partial.at[pl.ds(pl.multiple_of(c * chunk_rows + xx * block_rows, 16), block_rows), :],
                dst_ref=rs.at[c, j - 1], send_sem=send_sem.at[8 + part], recv_sem=rs_sem.at[unit],
                device_id={"shard": xx * 2 + yh}, device_id_type=MESH,
            ).start()

    def half_sums(part, c):
        partial, rs, yb, yr = sides[part][:4]
        unit = part * CHUNKS + c
        same_bytes(rs.at[c], rs_sem.at[unit]).wait()
        total = partial[own_rows(c), :].astype(f32)
        for j in range(3):
            total += rs[c, j].astype(f32)
        yb[c] = total.astype(bf16)
        pltpu.make_async_remote_copy(
            src_ref=yb.at[c], dst_ref=yr.at[c], send_sem=send_sem.at[10 + part], recv_sem=y_sem.at[unit],
            device_id={"shard": x * 2 + 1 - yh}, device_id_type=MESH,
        ).start()

    def activations(part, c):
        act, yb, yr = sides[part][4], sides[part][2], sides[part][3]
        unit = part * CHUNKS + c
        same_bytes(yr.at[c], y_sem.at[unit]).wait()
        gate_up = yb_gu[c].astype(f32) + yr_gu[c].astype(f32)
        gate, up = gate_up[:, :ff], gate_up[:, ff:]
        sigma = jax.nn.sigmoid(gate)
        active = gate * sigma
        here = own_rows(c)
        if part == 0:
            act[here, :] = (active * up).astype(bf16)
        else:
            grad_hidden = yb[c].astype(f32) + yr[c].astype(f32)
            act[here, :ff] = (grad_hidden * up * sigma * (1.0 + gate * (1.0 - sigma))).astype(bf16)
            act[here, ff:] = (grad_hidden * active).astype(bf16)
        for j in (2, 1, 3):
            xx = (x + j) % 4
            pltpu.make_async_remote_copy(
                src_ref=act.at[here, :], dst_ref=act.at[here, :], send_sem=send_sem.at[12 + part],
                recv_sem=ag_sem.at[unit], device_id={"shard": xx * 2 + yh}, device_id_type=MESH,
            ).start()

    def gathered(part, c):
        same_bytes(sides[part][5].at[c], ag_sem.at[part * CHUNKS + c]).wait()

    def row_grads(c):
        here = pl.ds(c * chunk_rows, chunk_rows)
        row_grad[here, :] = (
            jnp.dot(act_gu[here, :ff], weight[0], preferred_element_type=f32)
            + jnp.dot(act_gu[here, ff:], weight[1], preferred_element_type=f32)
        ).astype(bf16)

        def give_back(i, carry):
            rank, to_core = i // 2, i % 2
            dest = ((z + offset(16, rank)) % 16) * 2 + to_core
            src = row_grad.at[pl.ds(pl.multiple_of(i * CAP, CAP), CAP), :]
            dst = returned.at[pl.ds(pl.multiple_of(me * CAP, CAP), CAP), :]

            @pl.when(dest != me)
            def _():
                pltpu.make_async_remote_copy(
                    src_ref=src, dst_ref=dst, send_sem=send_sem.at[14], recv_sem=ret_sem,
                    device_id={"expert": dest}, device_id_type=MESH,
                ).start()

            @pl.when(dest == me)
            def _():
                pltpu.make_async_copy(src, dst, ret_sem).start()

            return carry

        lax.fori_loop(c * (n_owner // CHUNKS), (c + 1) * (n_owner // CHUNKS), give_back, 0)

    tn = (((0,), (0,)), ((), ()))
    pair_ff = 2 * part_ff

    def along_x(g):
        left, right = (
            (act_gu[:, g * ff : (g + 1) * ff], rows_in[:, :width])
            if g < 2
            else (act_hid[...], rows_in[:, width:])
        )
        wgrad[g] = lax.dot_general(left, right, tn, preferred_element_type=f32).astype(bf16)
        for j in (2, 1, 3):
            xx = (x + j) % 4
            pltpu.make_async_remote_copy(
                src_ref=wgrad.at[g, pl.ds(pl.multiple_of(xx * pair_ff, 16), pair_ff), :],
                dst_ref=turned.at[g, x], send_sem=send_sem.at[15], recv_sem=turn_sem.at[g],
                device_id={"shard": xx * 2 + yh}, device_id_type=MESH,
            ).start()
        pltpu.make_async_copy(
            wgrad.at[g, pl.ds(pl.multiple_of(x * pair_ff, 16), pair_ff), :], turned.at[g, x], turn_sem.at[g]
        ).start()

    def along_y(g):
        same_bytes(turned.at[g], turn_sem.at[g]).wait()

        def to_holder(i, c):
            to = (y + offset(8, i)) % 8
            h, q = to // 4, to % 4
            src = turned.at[g, q, pl.ds(pl.multiple_of(h * part_ff, 16), part_ff), :]
            dst = grads.at[g, y]

            @pl.when(to != y)
            def _():
                pltpu.make_async_remote_copy(
                    src_ref=src, dst_ref=dst, send_sem=send_sem.at[16], recv_sem=grad_sem.at[g],
                    device_id={"dp": q, "shard": x * 2 + h}, device_id_type=MESH,
                ).start()

            @pl.when(to == y)
            def _():
                pltpu.make_async_copy(src, dst, grad_sem.at[g]).start()

            return c

        lax.fori_loop(0, 8, to_holder, 0)

    units = [(part, c) for part in range(2) for c in range(CHUNKS)]
    for step in range(len(units) + LAG_ACT):
        if step == CHUNKS:
            same_bytes(weight.at[pl.ds(2, 1)], weight_sem.at[1]).wait()
        if step < len(units):
            products(*units[step])
        if 0 <= step - LAG_SUM < len(units):
            half_sums(*units[step - LAG_SUM])
        if 0 <= step - LAG_ACT:
            activations(*units[step - LAG_ACT])
        if step == AT_ONE:
            send_on(1)
        if step == AT_TURN:
            for c in range(CHUNKS):
                gathered(0, c)
            along_x(2)
        if step == AT_TWO:
            send_on(2)
    along_y(2)
    for c in range(CHUNKS - 1):
        gathered(1, c)
        row_grads(c)
    gathered(1, CHUNKS - 1)
    along_x(0)
    along_x(1)
    row_grads(CHUNKS - 1)
    along_y(0)
    along_y(1)

    same_bytes(returned, ret_sem).wait()
    token_grad_ref[...] = lax.dot_general(
        match[...], returned[...], tn, preferred_element_type=f32
    ).astype(bf16)

    same_bytes(moved.at[1], moved_sem.at[1]).wait()
    same_bytes(moved.at[2], moved_sem.at[2]).wait()
    for g in (2, 0, 1):
        same_bytes(grads.at[g], grad_sem.at[g]).wait()
        for h in range(2):
            half = slice(h * width, (h + 1) * width)
            gradient = grads[g, h * 4].astype(f32)
            for q in range(1, 4):
                gradient += grads[g, h * 4 + q].astype(f32)
            a, b, d = adamw_step(
                moved[0, g, :, half].astype(f32), moved[1, g, :, half].astype(f32),
                moved[2, g, :, half].astype(f32), gradient,
            )
            master_out_ref[0, g, :, half] = a
            first_out_ref[0, g, :, half] = b
            second_out_ref[0, g, :, half] = d

    for a in range(3):
        states_sent(a)
    same_bytes(rows_out.at[pl.ds(0, 31 * CAP)], send_sem.at[6]).wait()

    @pl.when(diagonal)
    def _():
        same_bytes(wgrad.at[:, pl.ds(0, 7 * part_ff), :], send_sem.at[7]).wait()

    @pl.when(jnp.logical_not(diagonal))
    def _():
        same_bytes(wgrad, send_sem.at[7]).wait()

    same_bytes(turned.at[:, pl.ds(0, 3)], send_sem.at[15]).wait()
    same_bytes(grads.at[:, pl.ds(0, 7)], send_sem.at[16]).wait()
    for part in range(2):
        same_bytes(sides[part][1], send_sem.at[8 + part]).wait()
        same_bytes(sides[part][2], send_sem.at[10 + part]).wait()
        same_bytes(sides[part][5], send_sem.at[12 + part]).wait()
    same_bytes(row_grad.at[pl.ds(0, 31 * CAP)], send_sem.at[14]).wait()


def on_device(
    tokens, out_grad, expert_ids, combine, old_place, new_place, master, moment_one, moment_two
):
    n_owner = 32
    owners = jnp.arange(n_owner, dtype=jnp.int32)
    holds = (new_place[:, None] == owners[None, :]).astype(jnp.int32)
    source_owner = jnp.sum(old_place[:, None] * holds, axis=0)
    tok, width = tokens.shape
    _, mats, part_ff, held_width = master.shape
    ff = part_ff * 8
    rows = n_owner * CAP
    block = rows // CHUNKS // 4
    vmem = pl.BlockSpec(memory_space=pltpu.VMEM)
    dma = pltpu.SemaphoreType.DMA
    return pl.pallas_call(
        kernel,
        out_shape=(
            jax.ShapeDtypeStruct(tokens.shape, bf16),
            jax.ShapeDtypeStruct(master.shape, f32),
            jax.ShapeDtypeStruct(master.shape, f32),
            jax.ShapeDtypeStruct(master.shape, f32),
        ),
        in_specs=[pl.BlockSpec(memory_space=pltpu.SMEM)] + [pl.BlockSpec(memory_space=pltpu.HBM)] * 8,
        out_specs=(vmem,) * 4,
        scratch_shapes=[
            pltpu.VMEM((1, n_owner), jnp.int32),
            pltpu.VMEM((1, tok), jnp.int32),
            pltpu.VMEM((1, tok), f32),
            pltpu.VMEM(tokens.shape, bf16),
            pltpu.VMEM(tokens.shape, bf16),
            pltpu.VMEM(master.shape, f32),
            pltpu.VMEM(master.shape, f32),
            pltpu.VMEM(master.shape, f32),
            pltpu.VMEM((rows, tok), bf16),
            pltpu.VMEM((rows, 2 * width), bf16),
            pltpu.VMEM((rows, 2 * width), bf16),
            pltpu.VMEM((3, mats, part_ff, held_width), bf16),
            pltpu.VMEM((n_owner, part_ff, 128), bf16),
            pltpu.VMEM((n_owner, part_ff, 128), bf16),
            pltpu.VMEM((n_owner, part_ff, 128), bf16),
            pltpu.VMEM((3, n_owner, part_ff, 128), bf16),
            pltpu.VMEM((3, mats, part_ff, held_width), bf16),
            pltpu.VMEM((mats, ff, width), bf16),
            pltpu.VMEM((rows, 2 * ff), bf16),
            pltpu.VMEM((rows, ff), bf16),
            pltpu.VMEM((CHUNKS, 3, block, 2 * ff), bf16),
            pltpu.VMEM((CHUNKS, 3, block, ff), bf16),
            pltpu.VMEM((CHUNKS, block, 2 * ff), bf16),
            pltpu.VMEM((CHUNKS, block, ff), bf16),
            pltpu.VMEM((CHUNKS, block, 2 * ff), bf16),
            pltpu.VMEM((CHUNKS, block, ff), bf16),
            pltpu.VMEM((rows, ff), bf16),
            pltpu.VMEM((rows, 2 * ff), bf16),
            pltpu.VMEM((rows, width), bf16),
            pltpu.VMEM((rows, width), bf16),
            pltpu.VMEM((mats, ff, width), bf16),
            pltpu.VMEM((mats, 4, 2 * part_ff, width), bf16),
            pltpu.VMEM((mats, 8, part_ff, width), bf16),
            dma((8,)),
            dma((17,)),
            dma((CHUNKS,)),
            dma((3,)),
            dma((3,)),
            dma((2,)),
            dma((2 * CHUNKS,)),
            dma((2 * CHUNKS,)),
            dma((2 * CHUNKS,)),
            dma,
            dma((3,)),
            dma((3,)),
        ],
        compiler_params=pltpu.CompilerParams(
            collective_id=0, has_side_effects=True, vmem_limit_bytes=60 * 1024 * 1024
        ),
    )(
        source_owner, new_place.reshape(1, n_owner), expert_ids.reshape(1, tok),
        combine.reshape(1, tok), tokens, out_grad, master, moment_one, moment_two,
    )


def solution(mesh):
    in_specs = (
        P(("dp", "expert"), "shard"),
        P(("dp", "expert"), "shard"),
        P(("dp", "expert"), None),
        P(("dp", "expert"), None),
        P(),
        P(),
        P("expert", None, "shard", "dp"),
        P("expert", None, "shard", "dp"),
        P("expert", None, "shard", "dp"),
    )
    out_specs = (
        P(("dp", "expert"), "shard"),
        P("expert", None, "shard", "dp"),
        P("expert", None, "shard", "dp"),
        P("expert", None, "shard", "dp"),
    )
    return jax.shard_map(
        on_device, mesh=mesh, in_specs=in_specs, out_specs=out_specs, check_vma=False
    )
```

```python
import functools

import jax
import jax.numpy as jnp
from jax import lax
from jax.experimental import pallas as pl
from jax.experimental.pallas import tpu as pltpu
from jax.sharding import PartitionSpec as P

MESH = pl.DeviceIdType.MESH
bf16 = jnp.bfloat16
f32 = jnp.float32

beta_first = 0.9
beta_second = 0.95
adam_epsilon = 1e-08
learn_rate = 0.001
weight_decay = 0.1
bias_first = 1.0 - beta_first**10
bias_second = 1.0 - beta_second**10

LAG_SUM, LAG_ACT = 4, 8
AT_ONE, AT_TWO, AT_TURN = 8, 10, 12
CHUNKS = 4
CAP = 16
PARKS = ((0, 0), (0, 1), (2, 0))


def same_bytes(ref, sem):
    return pltpu.make_async_copy(ref, ref, sem)


def adamw_step(master, moment_one, moment_two, gradient):
    first_out = beta_first * moment_one + (1.0 - beta_first) * gradient
    second_out = beta_second * moment_two + (1.0 - beta_second) * gradient * gradient
    update = first_out / bias_first / (jnp.sqrt(second_out / bias_second) + adam_epsilon)
    master_out = master - learn_rate * (update + weight_decay * master)
    return master_out, first_out, second_out


def kernel(
    source_ref, *refs,
):
    inputs, outputs, scratch = refs[:8], refs[8:12], refs[12:]
    body(source_ref, inputs, *outputs, *scratch)


def body(
    source_ref, inputs,
    token_grad_ref, master_out_ref, first_out_ref, second_out_ref,
    place_ref, ids_ref, combine_ref, tokens_ref, out_grad_ref, master_ref, one_ref, two_ref,
    match, rows_out, rows_in, states, parked_0, parked_1, parked_2, onward, moved,
    weight, partial_gu, partial_dn, rs_gu, rs_dn, yb_gu, yb_dn, yr_gu, yr_dn, act_hid, act_gu, row_grad, returned, wgrad, turned, grads,
    in_sem, send_sem, rows_sem, park_sem, moved_sem, weight_sem, rs_sem, y_sem, ag_sem, ret_sem, turn_sem, grad_sem,
):
    p = lax.axis_index("dp")
    me = lax.axis_index("expert")
    s = lax.axis_index("shard")
    z, core = me // 2, me % 2
    x, yh = s // 2, s % 2
    n_owner = 32
    n_rows = n_owner * CAP
    chunk_rows = n_rows // CHUNKS
    block_rows = chunk_rows // 4
    width = tokens_ref.shape[1]
    ff = weight.shape[1]
    part_ff = ff // 8

    y = yh * 4 + p
    parked = (parked_0, parked_1, parked_2)
    staged = (place_ref, ids_ref, combine_ref, tokens_ref, out_grad_ref, master_ref, one_ref, two_ref)

    def load(i):
        return pltpu.make_async_copy(inputs[i], staged[i], in_sem.at[i])

    for i in (5, 0, 1, 2, 3, 4, 6, 7):
        load(i).start()

    def offset(n, i):
        rank = n - 1 - i
        return jnp.where(rank % 2 == 1, (rank + 1) // 2, (n - rank // 2) % n)

    barrier = pltpu.get_barrier_semaphore()

    def greet(device):
        pl.semaphore_signal(barrier, inc=1, device_id=device, device_id_type=MESH)

    def greet_owner(i, c):
        greet({"expert": (me + i) % n_owner})
        return c

    lax.fori_loop(1, n_owner, greet_owner, 0)
    for j in (1, 2, 3):
        greet({"shard": ((x + j) % 4) * 2 + yh})

    def greet_y(i, c):
        to = (y + i) % 8
        greet({"dp": to % 4, "shard": x * 2 + to // 4})
        return c

    lax.fori_loop(1, 8, greet_y, 0)
    diagonal = x == p

    def greet_spread(i, c):
        h, q = i // 4, i % 4

        @pl.when(jnp.logical_or(q != p, p * 2 + h != s))
        def _():
            greet({"dp": q, "shard": p * 2 + h})

        @pl.when(jnp.logical_or(x != p, i != s))
        def _():
            greet({"dp": x, "shard": i})

        return c

    lax.fori_loop(0, 8, greet_spread, 0)
    load(5).wait()
    states[0] = master_ref[0].astype(bf16)
    pl.semaphore_wait(barrier, jnp.where(diagonal, 55, 57))

    def is_park(a):
        shift, c = PARKS[a]
        zz = (z + 16 - shift) % 16
        return jnp.logical_and(core == c, zz % 4 != 3), jnp.minimum(zz - zz // 4, 11)

    def park(a):
        shift, to_core = PARKS[a]

        def step(i, c):
            to = (z + offset(16, i)) % 16
            place_in = (to + 16 - shift) % 16
            k = jnp.minimum(place_in - place_in // 4, 11)
            g, lane = k // 4, pl.multiple_of((k % 4) * 128, 128)
            dest = 2 * to + to_core
            holds_one = place_in % 4 != 3
            src = states.at[a, g, :, pl.ds(lane, 128)]

            @pl.when(jnp.logical_and(holds_one, dest != me))
            def _():
                pltpu.make_async_remote_copy(
                    src_ref=src, dst_ref=parked[a].at[me], send_sem=send_sem.at[a],
                    recv_sem=park_sem.at[a], device_id={"expert": dest}, device_id_type=MESH,
                ).start()

            @pl.when(jnp.logical_and(holds_one, dest == me))
            def _():
                pltpu.make_async_copy(src, parked[a].at[me], park_sem.at[a]).start()

            return c

        lax.fori_loop(0, 16, step, 0)

    def send_on(a):
        mine, k = is_park(a)
        g, lane = k // 4, pl.multiple_of((k % 4) * 128, 128)

        @pl.when(mine)
        def _():
            same_bytes(parked[a], park_sem.at[a]).wait()

            def step(i, c):
                o = ((z + offset(16, i // 2)) % 16) * 2 + i % 2
                onward[a, o] = parked[a][source_ref[o]]
                dst = moved.at[a, g, :, pl.ds(lane, 128)]

                @pl.when(o != me)
                def _():
                    pltpu.make_async_remote_copy(
                        src_ref=onward.at[a, o], dst_ref=dst, send_sem=send_sem.at[3 + a],
                        recv_sem=moved_sem.at[a], device_id={"expert": o}, device_id_type=MESH,
                    ).start()

                @pl.when(o == me)
                def _():
                    pltpu.make_async_copy(onward.at[a, o], dst, moved_sem.at[a]).start()

                return c

            lax.fori_loop(0, n_owner, step, 0)

    def states_sent(a):
        mine, _ = is_park(a)

        @pl.when(mine)
        def _():
            same_bytes(onward.at[a, pl.ds(0, 11)], send_sem.at[a]).wait()
            same_bytes(onward.at[a, pl.ds(0, 31)], send_sem.at[3 + a]).wait()

        @pl.when(jnp.logical_not(mine))
        def _():
            same_bytes(onward.at[a, pl.ds(0, 12)], send_sem.at[a]).wait()

    park(0)

    for i in range(5):
        load(i).wait()
    tok = tokens_ref.shape[0]
    eye = lax.broadcasted_iota(jnp.int32, (n_owner, n_owner), 0) == lax.broadcasted_iota(
        jnp.int32, (n_owner, n_owner), 1
    )
    place = jnp.sum(jnp.where(eye, place_ref[...].astype(f32), 0.0), axis=1, keepdims=True)
    onehot = jnp.where(
        lax.broadcasted_iota(jnp.int32, (n_owner, tok), 0) == ids_ref[...], 1.0, 0.0
    )
    before = jnp.where(
        lax.broadcasted_iota(jnp.int32, (tok, tok), 0) < lax.broadcasted_iota(jnp.int32, (tok, tok), 1),
        1.0, 0.0,
    ).astype(bf16)
    earlier = jnp.dot(onehot.astype(bf16), before, preferred_element_type=f32)
    position = jnp.sum(onehot * (earlier + place * float(CAP)), axis=0, keepdims=True)
    chosen = lax.broadcasted_iota(jnp.int32, (n_rows, tok), 0).astype(f32) == position
    match[...] = jnp.where(chosen, 1.0, 0.0).astype(bf16)
    scale = jnp.sum(jnp.where(chosen, combine_ref[...], 0.0), axis=1, keepdims=True)
    rows_out[:, :width] = jnp.dot(match[...], tokens_ref[...], preferred_element_type=f32).astype(bf16)
    rows_out[:, width:] = (
        scale * jnp.dot(match[...], out_grad_ref[...], preferred_element_type=f32)
    ).astype(bf16)

    send_on(0)

    def dispatch(i, c):
        rank, to_core = i // 2, i % 2
        dest = ((z + 16 - offset(16, rank)) % 16) * 2 + to_core
        src = rows_out.at[pl.ds(pl.multiple_of(dest * CAP, CAP), CAP), :]
        dst = rows_in.at[pl.ds(pl.multiple_of((rank * 2 + core) * CAP, CAP), CAP), :]
        sem = rows_sem.at[rank // (16 // CHUNKS)]

        @pl.when(dest != me)
        def _():
            pltpu.make_async_remote_copy(
                src_ref=src, dst_ref=dst, send_sem=send_sem.at[6], recv_sem=sem,
                device_id={"expert": dest}, device_id_type=MESH,
            ).start()

        @pl.when(dest == me)
        def _():
            pltpu.make_async_copy(src, dst, sem).start()

        return c

    lax.fori_loop(0, n_owner, dispatch, 0)

    same_bytes(moved.at[0], moved_sem.at[0]).wait()

    def spread_part(part, i, c):
        to = (y + offset(8, i)) % 8
        h, q = to // 4, to % 4
        mats = pl.ds(0, 2) if part == 0 else pl.ds(2, 1)
        src = moved.at[0, mats, :, pl.ds(pl.multiple_of(h * width, width), width)]
        dst = weight.at[mats, pl.ds(pl.multiple_of(s * part_ff, 16), part_ff), :]
        away = jnp.logical_or(q != p, p * 2 + h != s)

        @pl.when(away)
        def _():
            pltpu.make_async_remote_copy(
                src_ref=src, dst_ref=dst, send_sem=send_sem.at[7], recv_sem=weight_sem.at[part],
                device_id={"dp": q, "shard": p * 2 + h}, device_id_type=MESH,
            ).start()

        @pl.when(jnp.logical_not(away))
        def _():
            pltpu.make_async_copy(src, dst, weight_sem.at[part]).start()

        return c

    lax.fori_loop(0, 8, functools.partial(spread_part, 0), 0)
    lax.fori_loop(0, 8, functools.partial(spread_part, 1), 0)
    load(6).wait()
    states[1] = one_ref[0].astype(bf16)
    park(1)
    load(7).wait()
    states[2] = two_ref[0].astype(bf16)
    park(2)
    same_bytes(weight.at[pl.ds(0, 2)], weight_sem.at[0]).wait()

    nt = (((1,), (1,)), ((), ()))

    def own_rows(c):
        return pl.ds(pl.multiple_of(c * chunk_rows + x * block_rows, 16), block_rows)

    sides = (
        (partial_gu, rs_gu, yb_gu, yr_gu, act_hid, rs_dn),
        (partial_dn, rs_dn, yb_dn, yr_dn, act_gu, rs_gu),
    )

    def products(part, c):
        partial, rs = sides[part][:2]
        unit = part * CHUNKS + c
        here = pl.ds(c * chunk_rows, chunk_rows)
        if part == 0:
            same_bytes(rows_in.at[here], rows_sem.at[c]).wait()
            for g in range(2):
                partial[here, g * ff : (g + 1) * ff] = lax.dot_general(
                    rows_in[here, :width], weight[g], nt, preferred_element_type=f32
                ).astype(bf16)
        else:
            partial[here, :] = lax.dot_general(
                rows_in[here, width:], weight[2], nt, preferred_element_type=f32
            ).astype(bf16)
        for j in (2, 1, 3):
            xx = (x + j) % 4
            pltpu.make_async_remote_copy(
                src_ref=partial.at[pl.ds(pl.multiple_of(c * chunk_rows + xx * block_rows, 16), block_rows), :],
                dst_ref=rs.at[c, j - 1], send_sem=send_sem.at[8 + part], recv_sem=rs_sem.at[unit],
                device_id={"shard": xx * 2 + yh}, device_id_type=MESH,
            ).start()

    def half_sums(part, c):
        partial, rs, yb, yr = sides[part][:4]
        unit = part * CHUNKS + c
        same_bytes(rs.at[c], rs_sem.at[unit]).wait()
        total = partial[own_rows(c), :].astype(f32)
        for j in range(3):
            total += rs[c, j].astype(f32)
        yb[c] = total.astype(bf16)
        pltpu.make_async_remote_copy(
            src_ref=yb.at[c], dst_ref=yr.at[c], send_sem=send_sem.at[10 + part], recv_sem=y_sem.at[unit],
            device_id={"shard": x * 2 + 1 - yh}, device_id_type=MESH,
        ).start()

    def activations(part, c):
        act, yb, yr = sides[part][4], sides[part][2], sides[part][3]
        unit = part * CHUNKS + c
        same_bytes(yr.at[c], y_sem.at[unit]).wait()
        gate_up = yb_gu[c].astype(f32) + yr_gu[c].astype(f32)
        gate, up = gate_up[:, :ff], gate_up[:, ff:]
        sigma = jax.nn.sigmoid(gate)
        active = gate * sigma
        here = own_rows(c)
        if part == 0:
            act[here, :] = (active * up).astype(bf16)
        else:
            grad_hidden = yb[c].astype(f32) + yr[c].astype(f32)
            act[here, :ff] = (grad_hidden * up * sigma * (1.0 + gate * (1.0 - sigma))).astype(bf16)
            act[here, ff:] = (grad_hidden * active).astype(bf16)
        for j in (2, 1, 3):
            xx = (x + j) % 4
            pltpu.make_async_remote_copy(
                src_ref=act.at[here, :], dst_ref=act.at[here, :], send_sem=send_sem.at[12 + part],
                recv_sem=ag_sem.at[unit], device_id={"shard": xx * 2 + yh}, device_id_type=MESH,
            ).start()

    def gathered(part, c):
        same_bytes(sides[part][5].at[c], ag_sem.at[part * CHUNKS + c]).wait()

    def row_grads(c):
        here = pl.ds(c * chunk_rows, chunk_rows)
        row_grad[here, :] = (
            jnp.dot(act_gu[here, :ff], weight[0], preferred_element_type=f32)
            + jnp.dot(act_gu[here, ff:], weight[1], preferred_element_type=f32)
        ).astype(bf16)

        def give_back(i, carry):
            rank, to_core = i // 2, i % 2
            dest = ((z + offset(16, rank)) % 16) * 2 + to_core
            src = row_grad.at[pl.ds(pl.multiple_of(i * CAP, CAP), CAP), :]
            dst = returned.at[pl.ds(pl.multiple_of(me * CAP, CAP), CAP), :]

            @pl.when(dest != me)
            def _():
                pltpu.make_async_remote_copy(
                    src_ref=src, dst_ref=dst, send_sem=send_sem.at[14], recv_sem=ret_sem,
                    device_id={"expert": dest}, device_id_type=MESH,
                ).start()

            @pl.when(dest == me)
            def _():
                pltpu.make_async_copy(src, dst, ret_sem).start()

            return carry

        lax.fori_loop(c * (n_owner // CHUNKS), (c + 1) * (n_owner // CHUNKS), give_back, 0)

    tn = (((0,), (0,)), ((), ()))
    pair_ff = 2 * part_ff

    def along_x(g):
        left, right = (
            (act_gu[:, g * ff : (g + 1) * ff], rows_in[:, :width])
            if g < 2
            else (act_hid[...], rows_in[:, width:])
        )
        wgrad[g] = lax.dot_general(left, right, tn, preferred_element_type=f32).astype(bf16)
        for j in (2, 1, 3):
            xx = (x + j) % 4
            pltpu.make_async_remote_copy(
                src_ref=wgrad.at[g, pl.ds(pl.multiple_of(xx * pair_ff, 16), pair_ff), :],
                dst_ref=turned.at[g, x], send_sem=send_sem.at[15], recv_sem=turn_sem.at[g],
                device_id={"shard": xx * 2 + yh}, device_id_type=MESH,
            ).start()
        pltpu.make_async_copy(
            wgrad.at[g, pl.ds(pl.multiple_of(x * pair_ff, 16), pair_ff), :], turned.at[g, x], turn_sem.at[g]
        ).start()

    def along_y(g):
        same_bytes(turned.at[g], turn_sem.at[g]).wait()

        def to_holder(i, c):
            to = (y + offset(8, i)) % 8
            h, q = to // 4, to % 4
            src = turned.at[g, q, pl.ds(pl.multiple_of(h * part_ff, 16), part_ff), :]
            dst = grads.at[g, y]

            @pl.when(to != y)
            def _():
                pltpu.make_async_remote_copy(
                    src_ref=src, dst_ref=dst, send_sem=send_sem.at[16], recv_sem=grad_sem.at[g],
                    device_id={"dp": q, "shard": x * 2 + h}, device_id_type=MESH,
                ).start()

            @pl.when(to == y)
            def _():
                pltpu.make_async_copy(src, dst, grad_sem.at[g]).start()

            return c

        lax.fori_loop(0, 8, to_holder, 0)

    units = [(part, c) for part in range(2) for c in range(CHUNKS)]
    for step in range(len(units) + LAG_ACT):
        if step == CHUNKS:
            same_bytes(weight.at[pl.ds(2, 1)], weight_sem.at[1]).wait()
        if step < len(units):
            products(*units[step])
        if 0 <= step - LAG_SUM < len(units):
            half_sums(*units[step - LAG_SUM])
        if 0 <= step - LAG_ACT:
            activations(*units[step - LAG_ACT])
        if step == AT_ONE:
            send_on(1)
        if step == AT_TURN:
            for c in range(CHUNKS):
                gathered(0, c)
            along_x(2)
        if step == AT_TWO:
            send_on(2)
    along_y(2)
    for c in range(CHUNKS - 1):
        gathered(1, c)
        row_grads(c)
    gathered(1, CHUNKS - 1)
    along_x(0)
    along_x(1)
    row_grads(CHUNKS - 1)
    along_y(0)
    along_y(1)

    same_bytes(moved.at[1], moved_sem.at[1]).wait()
    same_bytes(moved.at[2], moved_sem.at[2]).wait()
    for g in (2, 0, 1):
        same_bytes(grads.at[g], grad_sem.at[g]).wait()
        for h in range(2):
            half = slice(h * width, (h + 1) * width)
            gradient = grads[g, h * 4].astype(f32)
            for q in range(1, 4):
                gradient += grads[g, h * 4 + q].astype(f32)
            a, b, d = adamw_step(
                moved[0, g, :, half].astype(f32), moved[1, g, :, half].astype(f32),
                moved[2, g, :, half].astype(f32), gradient,
            )
            master_out_ref[0, g, :, half] = a
            first_out_ref[0, g, :, half] = b
            second_out_ref[0, g, :, half] = d

    same_bytes(returned, ret_sem).wait()
    token_grad_ref[...] = lax.dot_general(
        match[...], returned[...], tn, preferred_element_type=f32
    ).astype(bf16)

    for a in range(3):
        states_sent(a)
    same_bytes(rows_out.at[pl.ds(0, 31 * CAP)], send_sem.at[6]).wait()

    @pl.when(diagonal)
    def _():
        same_bytes(wgrad.at[:, pl.ds(0, 7 * part_ff), :], send_sem.at[7]).wait()

    @pl.when(jnp.logical_not(diagonal))
    def _():
        same_bytes(wgrad, send_sem.at[7]).wait()

    same_bytes(turned.at[:, pl.ds(0, 3)], send_sem.at[15]).wait()
    same_bytes(grads.at[:, pl.ds(0, 7)], send_sem.at[16]).wait()
    for part in range(2):
        same_bytes(sides[part][1], send_sem.at[8 + part]).wait()
        same_bytes(sides[part][2], send_sem.at[10 + part]).wait()
        same_bytes(sides[part][5], send_sem.at[12 + part]).wait()
    same_bytes(row_grad.at[pl.ds(0, 31 * CAP)], send_sem.at[14]).wait()


def on_device(
    tokens, out_grad, expert_ids, combine, old_place, new_place, master, moment_one, moment_two
):
    n_owner = 32
    owners = jnp.arange(n_owner, dtype=jnp.int32)
    holds = (new_place[:, None] == owners[None, :]).astype(jnp.int32)
    source_owner = jnp.sum(old_place[:, None] * holds, axis=0)
    tok, width = tokens.shape
    _, mats, part_ff, held_width = master.shape
    ff = part_ff * 8
    rows = n_owner * CAP
    block = rows // CHUNKS // 4
    vmem = pl.BlockSpec(memory_space=pltpu.VMEM)
    dma = pltpu.SemaphoreType.DMA
    return pl.pallas_call(
        kernel,
        out_shape=(
            jax.ShapeDtypeStruct(tokens.shape, bf16),
            jax.ShapeDtypeStruct(master.shape, f32),
            jax.ShapeDtypeStruct(master.shape, f32),
            jax.ShapeDtypeStruct(master.shape, f32),
        ),
        in_specs=[pl.BlockSpec(memory_space=pltpu.SMEM)] + [pl.BlockSpec(memory_space=pltpu.HBM)] * 8,
        out_specs=(vmem,) * 4,
        scratch_shapes=[
            pltpu.VMEM((1, n_owner), jnp.int32),
            pltpu.VMEM((1, tok), jnp.int32),
            pltpu.VMEM((1, tok), f32),
            pltpu.VMEM(tokens.shape, bf16),
            pltpu.VMEM(tokens.shape, bf16),
            pltpu.VMEM(master.shape, f32),
            pltpu.VMEM(master.shape, f32),
            pltpu.VMEM(master.shape, f32),
            pltpu.VMEM((rows, tok), bf16),
            pltpu.VMEM((rows, 2 * width), bf16),
            pltpu.VMEM((rows, 2 * width), bf16),
            pltpu.VMEM((3, mats, part_ff, held_width), bf16),
            pltpu.VMEM((n_owner, part_ff, 128), bf16),
            pltpu.VMEM((n_owner, part_ff, 128), bf16),
            pltpu.VMEM((n_owner, part_ff, 128), bf16),
            pltpu.VMEM((3, n_owner, part_ff, 128), bf16),
            pltpu.VMEM((3, mats, part_ff, held_width), bf16),
            pltpu.VMEM((mats, ff, width), bf16),
            pltpu.VMEM((rows, 2 * ff), bf16),
            pltpu.VMEM((rows, ff), bf16),
            pltpu.VMEM((CHUNKS, 3, block, 2 * ff), bf16),
            pltpu.VMEM((CHUNKS, 3, block, ff), bf16),
            pltpu.VMEM((CHUNKS, block, 2 * ff), bf16),
            pltpu.VMEM((CHUNKS, block, ff), bf16),
            pltpu.VMEM((CHUNKS, block, 2 * ff), bf16),
            pltpu.VMEM((CHUNKS, block, ff), bf16),
            pltpu.VMEM((rows, ff), bf16),
            pltpu.VMEM((rows, 2 * ff), bf16),
            pltpu.VMEM((rows, width), bf16),
            pltpu.VMEM((rows, width), bf16),
            pltpu.VMEM((mats, ff, width), bf16),
            pltpu.VMEM((mats, 4, 2 * part_ff, width), bf16),
            pltpu.VMEM((mats, 8, part_ff, width), bf16),
            dma((8,)),
            dma((17,)),
            dma((CHUNKS,)),
            dma((3,)),
            dma((3,)),
            dma((2,)),
            dma((2 * CHUNKS,)),
            dma((2 * CHUNKS,)),
            dma((2 * CHUNKS,)),
            dma,
            dma((3,)),
            dma((3,)),
        ],
        compiler_params=pltpu.CompilerParams(
            collective_id=0, has_side_effects=True, vmem_limit_bytes=60 * 1024 * 1024
        ),
    )(
        source_owner, new_place.reshape(1, n_owner), expert_ids.reshape(1, tok),
        combine.reshape(1, tok), tokens, out_grad, master, moment_one, moment_two,
    )


def solution(mesh):
    in_specs = (
        P(("dp", "expert"), "shard"),
        P(("dp", "expert"), "shard"),
        P(("dp", "expert"), None),
        P(("dp", "expert"), None),
        P(),
        P(),
        P("expert", None, "shard", "dp"),
        P("expert", None, "shard", "dp"),
        P("expert", None, "shard", "dp"),
    )
    out_specs = (
        P(("dp", "expert"), "shard"),
        P("expert", None, "shard", "dp"),
        P("expert", None, "shard", "dp"),
        P("expert", None, "shard", "dp"),
    )
    return jax.shard_map(
        on_device, mesh=mesh, in_specs=in_specs, out_specs=out_specs, check_vma=False
    )
```
